32 devices in a mesh: groups: 2 (over y), rep: 4 (over z), tp: 4 (over x, core).
Axes of the slice: x: 2, y: 2, z: 4, core: 2. Of those that a mesh axis runs over, the one named last changes fastest.
Arguments:
- row_states: bfloat16 [2, 64, 5120], P(None, ('groups', 'rep'), 'tp'), parts along dimension 1, may hold values from -6 to 6
- q_base: bfloat16 [2, 64, 8192], P(None, ('groups', 'rep'), 'tp'), parts along dimension 1, may hold values from -200 to 200
- cache_k: bfloat16 [2, 64, 384, 1024], P(None, ('groups', 'rep'), None, 'tp'), parts along dimension 1, may hold values from -8 to 8
- value_slots: bfloat16 [2, 64, 384, 1024], P(None, ('groups', 'rep'), None, 'tp'), parts along dimension 1, may hold values from -6 to 6
- current_key: bfloat16 [2, 64, 1024], P(None, ('groups', 'rep'), 'tp'), parts along dimension 1, may hold values from -6 to 6
- current_value: bfloat16 [2, 64, 1024], P(None, ('groups', 'rep'), 'tp'), parts along dimension 1, may hold values from -6 to 6
- cache_len: int32 [2, 64], P(None, ('groups', 'rep')), parts along dimension 1, may hold values from 2 to 384
- pool_a: bfloat16 [32, 32, 5120], P('rep', None, 'tp'), may hold values from -0.078125 to 0.078125
- pool_b: bfloat16 [32, 32, 8192], P('rep', None, 'tp'), may hold values from -1 to 1
- active_slots: int32 [2, 16], P(None, ('groups', 'rep')), parts along dimension 1, may hold values from 0 to 7, as said below
- row_adapter: int32 [2, 64, 1], P(None, ('groups', 'rep')), parts along dimension 1, may hold values from 0 to 7
Outputs:
- attended: bfloat16 [2, 64, 8192], P(None, ('groups', 'rep'), 'tp'), parts along dimension 1
The draws below stay inside these ranges and needn't reach their ends.
There are 2 independent parts, one for each index of `groups`. The reference program is written for one: setup_inputs(seed, part) draws one part's arguments, and reference() takes and returns one part's arrays. A program takes and returns all parts, laid end to end along the dimension named above; an argument that names none is the same for every part. Nothing has to cross between parts.
Inputs may be any that keep to these rules, and one draw needn't show every extreme that they name: `active_slots`: within each micro-batch, the 2 entries of one owner name distinct local pages.
All inputs are finite; a program needn't handle non-finite values.
Results may differ from the reference program's by a relative error of at most 0.0058.
Values may be sent and summed in bfloat16 or wider, within the bound.
A program may use at most 64 MiB of HBM per device.

```python
import jax
import jax.numpy as jnp
from jax import lax

D = 5120
QUERY_HEADS = 64
KEY_VALUE_HEADS = 8
HEAD_SIZE = 128
R = 32
ROW_BATCHES = 2
ACT_DEV = 2
ADP_DEV = 8
ROWS_DEV = 8
CONTEXT_SLOTS = 384
BATCH_ROWS = 32
ADAPTERS = 32
ACTIVE = 8
N_REP = 4


def draw_q_base(key, part):
    key = jax.random.fold_in(key, 11)
    unadapted = jax.random.normal(key, (ROW_BATCHES, BATCH_ROWS, QUERY_HEADS * HEAD_SIZE), jnp.float32)
    return jnp.clip(unadapted, -200.0, 200.0).astype(jnp.bfloat16)


def draw_cache_k(key, part):
    key = jax.random.fold_in(key, 13)
    unadapted = jax.random.normal(key, (ROW_BATCHES, BATCH_ROWS, CONTEXT_SLOTS, KEY_VALUE_HEADS * HEAD_SIZE), jnp.float32)
    return jnp.clip(unadapted, -8.0, 8.0).astype(jnp.bfloat16)


def draw_active_slots(key, part):
    key = jax.random.fold_in(key, 7)
    owners = ACTIVE // ACT_DEV
    owner_keys = jax.random.split(key, ROW_BATCHES * owners)
    orders = jax.vmap(lambda single: jax.random.permutation(single, ADP_DEV))(owner_keys)
    return orders[:, :ACT_DEV].reshape(ROW_BATCHES, ACTIVE).astype(jnp.int32)


def set_ends(result, stream_key, low, top_value):
    spot = [jax.random.randint(jax.random.fold_in(stream_key, axis), (), 0, length) for axis, length in enumerate(result.shape)]
    main_axis = result.shape.index(max(result.shape))
    neighbour = spot[:main_axis] + [(spot[main_axis] + 1) % result.shape[main_axis]] + spot[main_axis + 1:]
    return result.at[tuple(spot)].set(low).at[tuple(neighbour)].set(top_value)


def levels(own_key, shape, shards, low, largest):
    loudness, own = 1.0, jax.random.fold_in(own_key, 6)
    for dim, parts in shards:
        steps = jnp.exp(jax.random.uniform(jax.random.fold_in(own, dim), (parts,), jnp.float32, low / len(shards), largest / len(shards)))
        loudness = loudness * jnp.repeat(steps, shape[dim] // parts).reshape([-1 if axis == dim else 1 for axis in range(len(shape))])
    return loudness


def different_ones(own_key, rows, count, top, lift):
    ranking = jax.random.permutation(jax.random.fold_in(own_key, 1), count)
    pull = ranking
    for power in range(3):
        pull = pull * pull // count
    pull = pull * lift // count
    tickets = jax.random.randint(jax.random.fold_in(own_key, 2), (rows, count), 0, 4096) + pull
    fixed_rows = jax.random.permutation(jax.random.fold_in(own_key, 3), rows)[jnp.arange(count) % rows]
    tickets = jnp.where(jnp.arange(rows)[:, None] == fixed_rows[None, :], 1 << 14, tickets)
    priority = tickets * count + jnp.arange(count)
    return lax.top_k(priority.astype(jnp.int32), top)[1].astype(jnp.int32)


def centred(key, extent, scale, bound, cuts=(), held_as=jnp.bfloat16):
    result = jax.random.normal(key, extent, jnp.float32) * scale
    if len(cuts) > 0:
        result = levels(key, extent, cuts, -0.22, 0.18) * result
    return jnp.clip(result, min=-bound, max=bound).astype(held_as)


def setup_inputs(seed: int = 0, part: int = 0) -> dict:
    seeds = jax.random.split(jax.random.key(seed), 12)
    part_keys = jax.random.split(jax.random.fold_in(seeds[11], part), 12)
    row_states = centred(part_keys[0], (ROW_BATCHES, BATCH_ROWS, D), 1.0, 6.0, ((1, 4), (2, 4)))
    q_base = draw_q_base(jax.random.fold_in(jax.random.fold_in(seeds[11], part), 71), part)
    cache_k = draw_cache_k(jax.random.fold_in(jax.random.fold_in(seeds[11], part), 71), part)
    value_slots = centred(part_keys[3], (ROW_BATCHES, BATCH_ROWS, CONTEXT_SLOTS, KEY_VALUE_HEADS * HEAD_SIZE), 1.0, 6.0, ((1, 4), (3, 4)))
    current_key = centred(part_keys[4], (ROW_BATCHES, BATCH_ROWS, KEY_VALUE_HEADS * HEAD_SIZE), 1.0, 6.0, ((1, 4), (2, 4)))
    current_value = centred(part_keys[5], (ROW_BATCHES, BATCH_ROWS, KEY_VALUE_HEADS * HEAD_SIZE), 1.0, 6.0, ((1, 4), (2, 4)))
    cache_len = set_ends(jax.random.randint(part_keys[6], (ROW_BATCHES, BATCH_ROWS), 2, CONTEXT_SLOTS + 1), jax.random.fold_in(part_keys[6], 1), 2, CONTEXT_SLOTS).astype(jnp.int32)
    pool_a = centred(seeds[7], (ADAPTERS, R, D), D ** -0.5, 0.078125, ((0, 4), (2, 4)))
    pool_b = centred(seeds[8], (ADAPTERS, R, QUERY_HEADS * HEAD_SIZE), R ** -0.5, 1.0, ((0, 4), (2, 4)))
    active_slots = draw_active_slots(jax.random.fold_in(jax.random.fold_in(seeds[11], part), 71), part)
    row_adapter = different_ones(part_keys[10], ROW_BATCHES * BATCH_ROWS, ACTIVE, 1, 2048).reshape((ROW_BATCHES, BATCH_ROWS, 1))
    return {"row_states": row_states, "q_base": q_base, "cache_k": cache_k, "value_slots": value_slots, "current_key": current_key, "current_value": current_value, "cache_len": cache_len, "pool_a": pool_a, "pool_b": pool_b, "active_slots": active_slots, "row_adapter": row_adapter}


def attend_rows(query_rows, key_slots, value_slot_cache, token_key, token_value, lengths):
    number_rows = query_rows.shape[0]
    heads_per_group = QUERY_HEADS // KEY_VALUE_HEADS
    score_scale = HEAD_SIZE ** -0.5
    query_head_rows = query_rows.astype(jnp.float32).reshape(number_rows, KEY_VALUE_HEADS, heads_per_group, HEAD_SIZE)
    stored_keys = key_slots.astype(jnp.float32).reshape(number_rows, CONTEXT_SLOTS, KEY_VALUE_HEADS, HEAD_SIZE)
    stored_values = value_slot_cache.astype(jnp.float32).reshape(number_rows, CONTEXT_SLOTS, KEY_VALUE_HEADS, HEAD_SIZE)
    incoming_keys = token_key.astype(jnp.float32).reshape(number_rows, KEY_VALUE_HEADS, HEAD_SIZE)
    incoming_values = token_value.astype(jnp.float32).reshape(number_rows, KEY_VALUE_HEADS, HEAD_SIZE)
    scores = jnp.einsum("nhgd,nthd->nhgt", query_head_rows, stored_keys) * score_scale
    own_score = jnp.einsum("nhgd,nhd->nhg", query_head_rows, incoming_keys) * score_scale
    visible = jnp.arange(CONTEXT_SLOTS, dtype=jnp.int32)[None, :] < lengths[:, None]
    scores = jnp.where(visible[:, None, None, :], scores, -jnp.inf)
    highest = jnp.maximum(jnp.max(scores, axis=-1), own_score)
    weights = jnp.exp(scores - highest[..., None])
    own_weight = jnp.exp(own_score - highest)
    denominator = jnp.sum(weights, axis=-1) + own_weight
    weights_low = lax.optimization_barrier(weights.astype(jnp.bfloat16)).astype(jnp.float32)
    own_low = lax.optimization_barrier(own_weight.astype(jnp.bfloat16)).astype(jnp.float32)
    mixed = jnp.einsum("nhgt,nthd->nhgd", weights_low, stored_values)
    mixed = mixed + own_low[..., None] * incoming_values[:, :, None, :]
    return (mixed / denominator[..., None]).reshape(number_rows, QUERY_HEADS * HEAD_SIZE).astype(jnp.bfloat16)


def in_blocks(array):
    return array.reshape((N_REP, ROWS_DEV) + array.shape[1:])


def attend_block(arrays):
    return attend_rows(arrays[0], arrays[1], arrays[2], arrays[3], arrays[4], arrays[5])


def reference(row_states, q_base, cache_k, value_slots, current_key, current_value, cache_len, pool_a, pool_b, active_slots, row_adapter):
    outputs = []
    entries = jnp.arange(ACTIVE, dtype=jnp.int32)
    for step_index in range(ROW_BATCHES):
        page_index = (entries // ACT_DEV) * ADP_DEV + active_slots[step_index].astype(jnp.int32)
        shrink_pages = jnp.take(pool_a, page_index, axis=0).reshape(ACTIVE * R, D)
        expand_pages = jnp.take(pool_b, page_index, axis=0).reshape(ACTIVE * R, QUERY_HEADS * HEAD_SIZE)
        chooser = (row_adapter[step_index][:, 0:1] == entries[None, :]).astype(jnp.float32)
        product = jnp.dot(row_states[step_index], shrink_pages.T, preferred_element_type=jnp.float32).reshape(BATCH_ROWS, ACTIVE, R)
        shrink = jnp.sum(product * chooser[:, :, None], axis=1).astype(jnp.bfloat16)
        spread = (chooser[:, :, None].astype(jnp.bfloat16) * shrink[:, None, :]).reshape(BATCH_ROWS, ACTIVE * R)
        delta_rows = jnp.dot(spread, expand_pages, preferred_element_type=jnp.float32)
        query_rows = (q_base[step_index].astype(jnp.float32) + delta_rows).astype(jnp.bfloat16)
        attended = lax.map(attend_block, (in_blocks(query_rows), in_blocks(cache_k[step_index]), in_blocks(value_slots[step_index]), in_blocks(current_key[step_index]), in_blocks(current_value[step_index]), in_blocks(cache_len[step_index])))
        outputs.append(attended.reshape(BATCH_ROWS, QUERY_HEADS * HEAD_SIZE))
    return jnp.stack(outputs)
```

```python
import functools

import jax
import jax.numpy as jnp
from jax import lax
from jax.experimental import pallas as pl
from jax.experimental.pallas import tpu as pltpu
from jax.sharding import PartitionSpec as P

HEAD_SIZE = 128
HEADS_PER_GROUP = 8
LANES = 128
MESH = pl.DeviceIdType.MESH


def kernel(
    reps,
    tps,
    per_owner,
    rank,
    x_hbm,
    q_hbm,
    k_hbm,
    v_hbm,
    ck_hbm,
    cv_hbm,
    len_hbm,
    a_hbm,
    b_hbm,
    act_hbm,
    ad_hbm,
    out_hbm,
    xbuf,
    qbuf,
    kbuf,
    vbuf,
    ckbuf,
    cvbuf,
    abuf,
    bbuf,
    len_s,
    act_s,
    ad_s,
    pbuf,
    dsend,
    down,
    drecv,
    kcb,
    vcb,
    qs,
    os,
    obuf,
    load_sem,
    out_sem,
    x_send,
    x_recv,
    p_send,
    p_recv,
    d_send,
    d_recv,
):
    rows, features = x_hbm.shape
    half = rows // len_hbm.shape[0]
    slots = k_hbm.shape[1]
    page_lanes = a_hbm.shape[0]
    width = HEADS_PER_GROUP * HEAD_SIZE
    chunks = q_hbm.shape[1] // width
    lane_groups = LANES // rank
    lane_blocks = page_lanes // LANES
    sets = pbuf.shape[1]
    scale = HEAD_SIZE ** (-0.5)
    me = lax.axis_index("rep")
    mt = lax.axis_index("tp")

    def rep_at(step):
        return lax.rem(me + step + reps, reps)

    def tp_at(step):
        return lax.rem(mt + step, tps)

    barrier = pltpu.get_barrier_semaphore()
    for k in range(1, reps):
        pl.semaphore_signal(barrier, inc=1, device_id={"rep": rep_at(k)}, device_id_type=MESH)
    for j in range(1, tps):
        pl.semaphore_signal(barrier, inc=1, device_id={"tp": tp_at(j)}, device_id_type=MESH)

    pairs = [
        (ad_hbm, ad_s),
        (x_hbm, xbuf.at[0, :, pl.ds(0, features)]),
        (act_hbm, act_s),
        (a_hbm, abuf),
        (b_hbm, bbuf),
        (q_hbm, qbuf),
        (ck_hbm, ckbuf),
        (cv_hbm, cvbuf),
        (len_hbm, len_s),
        (k_hbm, kbuf),
        (v_hbm, vbuf),
    ]
    loads = [
        pltpu.make_async_copy(src, dst, load_sem.at[i]) for i, (src, dst) in enumerate(pairs)
    ]
    for load in loads:
        load.start()
    ld_ad, ld_x, ld_act, ld_a, ld_b, ld_q, ld_ck, ld_cv, ld_len, ld_k, ld_v = loads

    row_id = lax.broadcasted_iota(jnp.int32, (rows, LANES), 0)
    lane_group = lax.broadcasted_iota(jnp.int32, (rows, LANES), 1) // rank

    ld_ad.wait()
    entry = jnp.zeros((rows, LANES), jnp.int32)
    for n in range(rows):
        entry = jnp.where(row_id == n, ad_s[n // half, n % half], entry)
    xbuf[0, :, features:] = entry.astype(jnp.float32).astype(jnp.bfloat16)
    ld_x.wait()

    pl.semaphore_wait(barrier, reps - 1 + tps - 1)

    x_copies = []
    for k in range(1, reps):
        copy = pltpu.make_async_remote_copy(
            src_ref=xbuf.at[0],
            dst_ref=xbuf.at[k],
            send_sem=x_send.at[k],
            recv_sem=x_recv.at[k],
            device_id={"rep": rep_at(k)},
            device_id_type=MESH,
        )
        copy.start()
        x_copies.append(copy)

    ld_act.wait()
    slot_of = []
    for c in range(per_owner):
        slot = jnp.zeros((rows, LANES), jnp.int32)
        for w in range(len_hbm.shape[0]):
            slot = jnp.where(row_id // half == w, act_s[w, c], slot)
        slot_of.append(slot.astype(jnp.float32))

    ld_a.wait()

    def shrink_dot(block):
        return lax.dot_general(
            block, abuf[...], (((1,), (1,)), ((), ())), preferred_element_type=jnp.float32
        )

    own_product = shrink_dot(xbuf[0, :, :features])

    ld_ck.wait()
    ld_cv.wait()
    for c in range(chunks):
        head = slice(c * HEAD_SIZE, (c + 1) * HEAD_SIZE)
        keys = ckbuf[:, head].astype(jnp.float32)
        values = cvbuf[:, head].astype(jnp.float32)
        for n in range(rows):
            place = slice(n * HEADS_PER_GROUP, (n + 1) * HEADS_PER_GROUP)
            shape = (HEADS_PER_GROUP, HEAD_SIZE)
            kcb[c, place, :] = jnp.broadcast_to(keys[n : n + 1, :], shape)
            vcb[c, place, :] = jnp.broadcast_to(values[n : n + 1, :], shape)

    for copy in x_copies:
        copy.wait_recv()
    others = shrink_dot(xbuf[1:, :, :features].reshape((reps - 1) * rows, features))

    pages = []
    packed = [jnp.zeros((rows, LANES), jnp.float32) for _ in range(sets)]
    group_f = lane_group.astype(jnp.float32)
    for k in range(reps):
        product = own_product if k == 0 else others[(k - 1) * rows : k * rows]
        entry_k = xbuf[k, :, features:].astype(jnp.float32)
        page = jnp.full((rows, LANES), -1.0, jnp.float32)
        for c in range(per_owner):
            mine = (me * per_owner + c).astype(jnp.float32)
            page = jnp.where(entry_k == mine, slot_of[c], page)
        pages.append(page)
        kept = jnp.zeros((rows, LANES), jnp.float32)
        for b in range(lane_blocks):
            kept = kept + jnp.where(
                page == group_f + float(b * lane_groups), product[:, b * LANES : (b + 1) * LANES], 0.0
            )
        turn = LANES // 2
        while turn >= rank:
            kept = kept + pltpu.roll(kept, turn, 1)
            turn //= 2
        s, g = divmod(k, lane_groups)
        packed[s] = jnp.where(lane_group == g, kept, packed[s])
    for s in range(sets):
        pbuf[0, s] = packed[s]

    p_copies = []
    for j in range(1, tps):
        copy = pltpu.make_async_remote_copy(
            src_ref=pbuf.at[0],
            dst_ref=pbuf.at[j],
            send_sem=p_send.at[j],
            recv_sem=p_recv.at[j],
            device_id={"tp": tp_at(j)},
            device_id_type=MESH,
        )
        copy.start()
        p_copies.append(copy)
    ld_b.wait()
    for copy in p_copies:
        copy.wait_recv()

    spread = []
    for k in range(reps):
        s, g = divmod(k, lane_groups)
        if g == 0:
            total = pbuf[0, s]
            for j in range(1, tps):
                total = total + pbuf[j, s]
        shrink = jnp.where(lane_group == g, total, 0.0)
        turn = LANES // 2
        while turn >= rank:
            shrink = shrink + pltpu.roll(shrink, turn, 1)
            turn //= 2
        spread.append(
            jnp.concatenate(
                [
                    jnp.where(pages[k] == group_f + float(b * lane_groups), shrink, 0.0)
                    for b in range(lane_blocks)
                ],
                axis=1,
            ).astype(jnp.bfloat16)
        )
    spread = jnp.concatenate(spread, axis=0)

    d_copies = []
    for c in range(chunks):
        delta = jnp.dot(
            spread, bbuf[:, c * width : (c + 1) * width], preferred_element_type=jnp.float32
        )
        down[c] = delta[:rows]
        here = []
        for k in range(1, reps):
            dsend[c, k] = delta[k * rows : (k + 1) * rows].astype(jnp.bfloat16)
            copy = pltpu.make_async_remote_copy(
                src_ref=dsend.at[c, k],
                dst_ref=drecv.at[c, k],
                send_sem=d_send.at[c, k],
                recv_sem=d_recv.at[c, k],
                device_id={"rep": rep_at(-k)},
                device_id_type=MESH,
            )
            copy.start()
            here.append(copy)
        d_copies.append(here)

    ld_q.wait()
    ld_len.wait()
    ld_k.wait()
    ld_v.wait()
    slot_id = lax.broadcasted_iota(jnp.int32, (HEADS_PER_GROUP, slots), 1)
    out_copies = []
    for c in range(chunks):
        cols = slice(c * width, (c + 1) * width)
        head = slice(c * HEAD_SIZE, (c + 1) * HEAD_SIZE)
        for copy in d_copies[c]:
            copy.wait_recv()
        delta = down[c]
        for k in range(1, reps):
            delta = delta + drecv[c, k].astype(jnp.float32)
        queries = (qbuf[:, cols].astype(jnp.float32) + delta).astype(jnp.bfloat16)
        queries = queries.astype(jnp.float32)
        for h in range(HEADS_PER_GROUP):
            qs[pl.ds(h, rows, stride=HEADS_PER_GROUP), :] = queries[
                :, h * HEAD_SIZE : (h + 1) * HEAD_SIZE
            ]
        scores, owns = [], []
        for n in range(rows):
            place = slice(n * HEADS_PER_GROUP, (n + 1) * HEADS_PER_GROUP)
            query = qs[place, :]
            score = lax.dot_general(
                query.astype(jnp.bfloat16),
                kbuf[n, :, head],
                (((1,), (1,)), ((), ())),
                preferred_element_type=jnp.float32,
            )
            owns.append(jnp.sum(query * kcb[c, place, :], axis=1, keepdims=True) * scale)
            length = len_s[n // half, n % half]
            scores.append(jnp.where(slot_id < length, score * scale, -jnp.inf))
        weights, own_weights, denominators = [], [], []
        for n in range(rows):
            highest = jnp.maximum(jnp.max(scores[n], axis=1, keepdims=True), owns[n])
            weight = jnp.exp(scores[n] - highest)
            own_weight = jnp.exp(owns[n] - highest)
            denominators.append(jnp.sum(weight, axis=1, keepdims=True) + own_weight)
            weights.append(weight.astype(jnp.bfloat16))
            own_weights.append(own_weight.astype(jnp.bfloat16).astype(jnp.float32))
        for n in range(rows):
            place = slice(n * HEADS_PER_GROUP, (n + 1) * HEADS_PER_GROUP)
            mixed = jnp.dot(weights[n], vbuf[n, :, head], preferred_element_type=jnp.float32)
            mixed = mixed + own_weights[n] * vcb[c, place, :]
            os[place, :] = mixed / denominators[n]
        for h in range(HEADS_PER_GROUP):
            obuf[:, c * width + h * HEAD_SIZE : c * width + (h + 1) * HEAD_SIZE] = os[
                pl.ds(h, rows, stride=HEADS_PER_GROUP), :
            ].astype(jnp.bfloat16)
        copy = pltpu.make_async_copy(
            obuf.at[:, pl.ds(c * width, width)],
            out_hbm.at[:, pl.ds(c * width, width)],
            out_sem.at[c],
        )
        copy.start()
        out_copies.append(copy)

    for copy in x_copies + p_copies:
        copy.wait_send()
    for here in d_copies:
        for copy in here:
            copy.wait_send()
    for copy in out_copies:
        copy.wait()


def body(
    reps,
    tps,
    row_states,
    q_base,
    cache_k,
    value_slots,
    current_key,
    current_value,
    cache_len,
    pool_a,
    pool_b,
    active_slots,
    row_adapter,
):
    batches, each, features = row_states.shape
    rows = batches * each
    columns = q_base.shape[2]
    slots, kv_width = cache_k.shape[2:]
    pages, rank = pool_a.shape[:2]
    width = HEADS_PER_GROUP * HEAD_SIZE
    chunks = columns // width
    sets = -(-reps * rank // LANES)
    bf16, f32 = jnp.bfloat16, jnp.float32
    dma = pltpu.SemaphoreType.DMA
    scratch = [
        pltpu.VMEM((reps, rows, features + LANES), bf16),
        pltpu.VMEM((rows, columns), bf16),
        pltpu.VMEM((rows, slots, kv_width), bf16),
        pltpu.VMEM((rows, slots, kv_width), bf16),
        pltpu.VMEM((rows, kv_width), bf16),
        pltpu.VMEM((rows, kv_width), bf16),
        pltpu.VMEM((pages * rank, features), bf16),
        pltpu.VMEM((pages * rank, columns), bf16),
        pltpu.SMEM(cache_len.shape, jnp.int32),
        pltpu.SMEM(active_slots.shape, jnp.int32),
        pltpu.SMEM((batches, each), jnp.int32),
        pltpu.VMEM((tps, sets, rows, LANES), f32),
        pltpu.VMEM((chunks, reps, rows, width), bf16),
        pltpu.VMEM((chunks, rows, width), f32),
        pltpu.VMEM((chunks, reps, rows, width), bf16),
        pltpu.VMEM((chunks, rows * HEADS_PER_GROUP, HEAD_SIZE), f32),
        pltpu.VMEM((chunks, rows * HEADS_PER_GROUP, HEAD_SIZE), f32),
        pltpu.VMEM((rows * HEADS_PER_GROUP, HEAD_SIZE), f32),
        pltpu.VMEM((rows * HEADS_PER_GROUP, HEAD_SIZE), f32),
        pltpu.VMEM((rows, columns), bf16),
        dma((11,)),
        dma((chunks,)),
        dma((reps,)),
        dma((reps,)),
        dma((tps,)),
        dma((tps,)),
        dma((chunks, reps)),
        dma((chunks, reps)),
    ]
    anywhere = pl.BlockSpec(memory_space=pl.ANY)
    out = pl.pallas_call(
        functools.partial(kernel, reps, tps, active_slots.shape[1], rank),
        out_shape=jax.ShapeDtypeStruct((rows, columns), bf16),
        in_specs=[anywhere] * 11,
        out_specs=anywhere,
        scratch_shapes=scratch,
        compiler_params=pltpu.CompilerParams(
            collective_id=0, has_side_effects=True, vmem_limit_bytes=60 * 1024 * 1024
        ),
    )(
        row_states.reshape(rows, features),
        q_base.reshape(rows, columns),
        cache_k.reshape(rows, slots, kv_width),
        value_slots.reshape(rows, slots, kv_width),
        current_key.reshape(rows, kv_width),
        current_value.reshape(rows, kv_width),
        cache_len,
        pool_a.reshape(pages * rank, features),
        pool_b.reshape(pages * rank, columns),
        active_slots,
        row_adapter.reshape(batches, each),
    )
    return out.reshape(batches, each, columns)


def solution(mesh):
    placed = (
        P(None, ("groups", "rep"), "tp"),
        P(None, ("groups", "rep"), "tp"),
        P(None, ("groups", "rep"), None, "tp"),
        P(None, ("groups", "rep"), None, "tp"),
        P(None, ("groups", "rep"), "tp"),
        P(None, ("groups", "rep"), "tp"),
        P(None, ("groups", "rep")),
        P("rep", None, "tp"),
        P("rep", None, "tp"),
        P(None, ("groups", "rep")),
        P(None, ("groups", "rep"), None),
    )
    return jax.shard_map(
        functools.partial(body, mesh.shape["rep"], mesh.shape["tp"]),
        mesh=mesh,
        in_specs=placed,
        out_specs=P(None, ("groups", "rep"), "tp"),
        check_vma=False,
    )
```

```python
import functools

import jax
import jax.numpy as jnp
from jax import lax
from jax.experimental import pallas as pl
from jax.experimental.pallas import tpu as pltpu
from jax.sharding import PartitionSpec as P

HEAD_SIZE = 128
HEADS_PER_GROUP = 8
LANES = 128
MESH = pl.DeviceIdType.MESH


def kernel(
    reps,
    tps,
    per_owner,
    rank,
    x_hbm,
    q_hbm,
    k_hbm,
    v_hbm,
    ck_hbm,
    cv_hbm,
    len_hbm,
    a_hbm,
    b_hbm,
    act_hbm,
    ad_hbm,
    out_hbm,
    xbuf,
    qbuf,
    kbuf,
    vbuf,
    ckbuf,
    cvbuf,
    abuf,
    bbuf,
    len_s,
    act_s,
    ad_s,
    xs,
    pbuf,
    dsend,
    down,
    drecv,
    kcb,
    vcb,
    qs,
    os,
    wide_out,
    obuf,
    load_sem,
    out_sem,
    x_send,
    x_recv,
    p_send,
    p_recv,
    d_send,
    d_recv,
):
    rows, features = x_hbm.shape
    half = rows // len_hbm.shape[0]
    slots = k_hbm.shape[1]
    page_lanes = a_hbm.shape[0]
    width = HEADS_PER_GROUP * HEAD_SIZE
    chunks = q_hbm.shape[1] // width
    lane_groups = LANES // rank
    lane_blocks = page_lanes // LANES
    batches = len_hbm.shape[0]
    sets = pbuf.shape[2]
    fold = xbuf.shape[3]
    side_width = chunks * width // 2
    rest = features - fold
    scale = HEAD_SIZE ** (-0.5)
    last = reps - 1
    me = lax.axis_index("rep")
    mt = lax.axis_index("tp")

    def tp_at(step):
        return lax.rem(mt + step, tps)

    barrier = pltpu.get_barrier_semaphore()
    for k in range(1, reps):
        pl.semaphore_signal(
            barrier, inc=1, device_id={"rep": lax.rem(me + k, reps)}, device_id_type=MESH
        )
    for j in range(1, tps):
        pl.semaphore_signal(barrier, inc=1, device_id={"tp": tp_at(j)}, device_id_type=MESH)

    pairs = [
        (ad_hbm, ad_s),
        (x_hbm, xs),
        (act_hbm, act_s),
        (a_hbm, abuf),
        (b_hbm, bbuf),
        (q_hbm, qbuf),
        (ck_hbm, ckbuf),
        (cv_hbm, cvbuf),
        (len_hbm, len_s),
        (k_hbm, kbuf),
        (v_hbm, vbuf),
    ]
    loads = [
        pltpu.make_async_copy(src, dst, load_sem.at[i]) for i, (src, dst) in enumerate(pairs)
    ]
    for load in loads:
        load.start()
    ld_ad, ld_x, ld_act, ld_a, ld_b, ld_q, ld_ck, ld_cv, ld_len, ld_k, ld_v = loads

    row_id = lax.broadcasted_iota(jnp.int32, (rows, LANES), 0)
    lane_group = lax.broadcasted_iota(jnp.int32, (half, LANES), 1) // rank

    ld_ad.wait()
    entry = jnp.zeros((rows, LANES), jnp.int32)
    for n in range(rows):
        entry = jnp.where(row_id == n, ad_s[n // half, n % half], entry)
    entry = entry.astype(jnp.float32)
    ld_x.wait()
    for w in range(batches):
        mine = slice(w * half, (w + 1) * half)
        states = xs[...].astype(jnp.float32)[mine]
        below = [states[:, fold:], entry[mine]]
        if rest + LANES < fold:
            below.append(jnp.zeros((half, fold - rest - LANES), jnp.float32))
        folded = jnp.concatenate([states[:, :fold], jnp.concatenate(below, axis=1)], axis=0)
        xbuf[w, me] = folded.astype(jnp.bfloat16)

    pl.semaphore_wait(barrier, last + tps - 1)

    def reaches(side, step):
        return me + step <= last if side > 0 else me - step >= 0

    def arrives(side, step):
        return me - step >= 0 if side > 0 else me + step <= last

    def row_copy(w, side, step, peer, slot):
        return pltpu.make_async_remote_copy(
            src_ref=xbuf.at[w, slot],
            dst_ref=xbuf.at[w, slot],
            send_sem=x_send.at[w, (side + 1) // 2, step],
            recv_sem=x_recv.at[w, (side + 1) // 2, step],
            device_id={"rep": peer},
            device_id_type=MESH,
        )

    for w in range(batches):
        for step in range(last, 0, -1):
            for side in (1, -1):

                @pl.when(reaches(side, step))
                def _():
                    row_copy(w, side, step, me + side * step, me).start()

    for w in range(batches):
        drecv[w, me] = jnp.zeros((rows, side_width), jnp.bfloat16)

    ld_act.wait()
    ld_a.wait()

    def shrink_dot(block):
        return lax.dot_general(
            block, abuf[...], (((1,), (1,)), ((), ())), preferred_element_type=jnp.float32
        )

    ld_ck.wait()
    ld_cv.wait()
    for c in range(chunks):
        head = slice(c * HEAD_SIZE, (c + 1) * HEAD_SIZE)
        keys = ckbuf[:, head].astype(jnp.float32)
        values = cvbuf[:, head].astype(jnp.float32)
        for n in range(rows):
            place = slice(n * HEADS_PER_GROUP, (n + 1) * HEADS_PER_GROUP)
            shape = (HEADS_PER_GROUP, HEAD_SIZE)
            kcb[c, place, :] = jnp.broadcast_to(keys[n : n + 1, :], shape)
            vcb[c, place, :] = jnp.broadcast_to(values[n : n + 1, :], shape)

    group_f = lane_group.astype(jnp.float32)
    ld_b.wait()

    def shrink_part(w):
        for step in range(1, reps):
            for side in (1, -1):

                @pl.when(arrives(side, step))
                def _():
                    row_copy(w, side, step, me - side * step, me - side * step).wait_recv()

        states, entries = [], []
        for k in range(reps):
            folded = xbuf[w, k].astype(jnp.float32)
            states.append(jnp.concatenate([folded[:half], folded[half:, :rest]], axis=1))
            entries.append(folded[half:, rest : rest + LANES])
        products = shrink_dot(jnp.concatenate(states, axis=0).astype(jnp.bfloat16))
        pages = []
        packed = [jnp.zeros((half, LANES), jnp.float32) for _ in range(sets)]
        for k in range(reps):
            product = products[k * half : (k + 1) * half]
            page = jnp.full((half, LANES), -1.0, jnp.float32)
            for c in range(per_owner):
                mine = (me * per_owner + c).astype(jnp.float32)
                page = jnp.where(entries[k] == mine, act_s[w, c].astype(jnp.float32), page)
            pages.append(page)
            kept = jnp.zeros((half, LANES), jnp.float32)
            for b in range(lane_blocks):
                kept = kept + jnp.where(
                    page == group_f + float(b * lane_groups),
                    product[:, b * LANES : (b + 1) * LANES],
                    0.0,
                )
            turn = LANES // 2
            while turn >= rank:
                kept = kept + pltpu.roll(kept, turn, 1)
                turn //= 2
            s, g = divmod(k, lane_groups)
            packed[s] = jnp.where(lane_group == g, kept, packed[s])
        for s in range(sets):
            pbuf[w, 0, s] = packed[s]
        copies = []
        for j in range(1, tps):
            copy = pltpu.make_async_remote_copy(
                src_ref=pbuf.at[w, 0],
                dst_ref=pbuf.at[w, j],
                send_sem=p_send.at[w, j],
                recv_sem=p_recv.at[w, j],
                device_id={"tp": tp_at(j)},
                device_id_type=MESH,
            )
            copy.start()
            copies.append(copy)
        return pages, copies

    def delta_copy(w, side, step, peer, slot):
        return pltpu.make_async_remote_copy(
            src_ref=dsend.at[w, peer],
            dst_ref=drecv.at[w, slot],
            send_sem=d_send.at[w, (side + 1) // 2, step],
            recv_sem=d_recv.at[w, (side + 1) // 2, step],
            device_id={"rep": peer},
            device_id_type=MESH,
        )

    def expand_part(w, pages, copies):
        for copy in copies:
            copy.wait_recv()
        spread = []
        for k in range(reps):
            s, g = divmod(k, lane_groups)
            if g == 0:
                total = pbuf[w, 0, s]
                for j in range(1, tps):
                    total = total + pbuf[w, j, s]
            shrink = jnp.where(lane_group == g, total, 0.0)
            turn = LANES // 2
            while turn >= rank:
                shrink = shrink + pltpu.roll(shrink, turn, 1)
                turn //= 2
            spread.append(
                jnp.concatenate(
                    [
                        jnp.where(pages[k] == group_f + float(b * lane_groups), shrink, 0.0)
                        for b in range(lane_blocks)
                    ],
                    axis=1,
                )
            )
        spread = jnp.concatenate(spread, axis=0).astype(jnp.bfloat16)
        sides = [
            jnp.dot(
                spread,
                bbuf[:, i * side_width : (i + 1) * side_width],
                preferred_element_type=jnp.float32,
            )
            for i in range(2)
        ]
        for k in range(reps):
            block = jnp.concatenate([side[k * half : (k + 1) * half] for side in sides], axis=0)
            down[w, k] = block
            dsend[w, k] = block.astype(jnp.bfloat16)
        for step in range(last, 0, -1):
            for side in (1, -1):

                @pl.when(reaches(side, step))
                def _():
                    delta_copy(w, side, step, me + side * step, me).start()

    shrunk = [shrink_part(w) for w in range(batches)]
    for w in range(batches):
        expand_part(w, *shrunk[w])

    ld_q.wait()
    ld_len.wait()
    ld_k.wait()
    ld_v.wait()
    slot_id = lax.broadcasted_iota(jnp.int32, (HEADS_PER_GROUP, slots), 1)
    for w in range(batches):
        for step in range(1, reps):
            for side in (1, -1):

                @pl.when(arrives(side, step))
                def _():
                    delta_copy(w, side, step, me - side * step, me - side * step).wait_recv()

        delta = down[w, me]
        for k in range(reps):
            delta = delta + drecv[w, k].astype(jnp.float32)
        delta = jnp.concatenate([delta[:half], delta[half:]], axis=1)
        base = qbuf[...].astype(jnp.float32)[w * half : (w + 1) * half]
        queries = (base + delta).astype(jnp.bfloat16).astype(jnp.float32)
        pairs = [(c, n) for c in range(chunks) for n in range(half)]

        def place(c, n):
            start = (c * half + n) * HEADS_PER_GROUP
            return slice(start, start + HEADS_PER_GROUP)

        def wide(n):
            start = (w * half + n) * HEADS_PER_GROUP
            return slice(start, start + HEADS_PER_GROUP)

        for c in range(chunks):
            for h in range(HEADS_PER_GROUP):
                first = c * width + h * HEAD_SIZE
                qs[pl.ds(c * half * HEADS_PER_GROUP + h, half, stride=HEADS_PER_GROUP), :] = queries[
                    :, first : first + HEAD_SIZE
                ]
        scores, owns = [], []
        for c, n in pairs:
            query = qs[place(c, n), :]
            score = lax.dot_general(
                query.astype(jnp.bfloat16),
                kbuf[w * half + n, :, c * HEAD_SIZE : (c + 1) * HEAD_SIZE],
                (((1,), (1,)), ((), ())),
                preferred_element_type=jnp.float32,
            )
            owns.append(jnp.sum(query * kcb[c, wide(n), :], axis=1, keepdims=True) * scale)
            scores.append(jnp.where(slot_id < len_s[w, n], score * scale, -jnp.inf))
        weights, own_weights, denominators = [], [], []
        for score, own in zip(scores, owns):
            highest = jnp.maximum(jnp.max(score, axis=1, keepdims=True), own)
            weight = jnp.exp(score - highest)
            own_weight = jnp.exp(own - highest)
            denominators.append(jnp.sum(weight, axis=1, keepdims=True) + own_weight)
            weights.append(weight.astype(jnp.bfloat16))
            own_weights.append(own_weight.astype(jnp.bfloat16).astype(jnp.float32))
        for i, (c, n) in enumerate(pairs):
            mixed = jnp.dot(
                weights[i],
                vbuf[w * half + n, :, c * HEAD_SIZE : (c + 1) * HEAD_SIZE],
                preferred_element_type=jnp.float32,
            )
            mixed = mixed + own_weights[i] * vcb[c, wide(n), :]
            os[place(c, n), :] = mixed / denominators[i]
        for c in range(chunks):
            for h in range(HEADS_PER_GROUP):
                first = c * width + h * HEAD_SIZE
                wide_out[w * half : (w + 1) * half, first : first + HEAD_SIZE] = os[
                    pl.ds(c * half * HEADS_PER_GROUP + h, half, stride=HEADS_PER_GROUP), :
                ]
    obuf[...] = wide_out[...].astype(jnp.bfloat16)
    out_copy = pltpu.make_async_copy(obuf, out_hbm, out_sem)
    out_copy.start()

    for _, copies in shrunk:
        for copy in copies:
            copy.wait_send()
    for step in range(1, reps):
        for side in (1, -1):

            @pl.when(reaches(side, step))
            def _():
                for w in range(batches):
                    row_copy(w, side, step, me + side * step, me).wait_send()
                    delta_copy(w, side, step, me + side * step, me).wait_send()

    out_copy.wait()


def body(
    reps,
    tps,
    row_states,
    q_base,
    cache_k,
    value_slots,
    current_key,
    current_value,
    cache_len,
    pool_a,
    pool_b,
    active_slots,
    row_adapter,
):
    batches, each, features = row_states.shape
    rows = batches * each
    columns = q_base.shape[2]
    slots, kv_width = cache_k.shape[2:]
    pages, rank = pool_a.shape[:2]
    width = HEADS_PER_GROUP * HEAD_SIZE
    chunks = columns // width
    sets = -(-reps * rank // LANES)
    fold = (features + 2 * LANES) // (2 * LANES) * LANES
    bf16, f32 = jnp.bfloat16, jnp.float32
    dma = pltpu.SemaphoreType.DMA
    scratch = [
        pltpu.VMEM((batches, reps, rows, fold), bf16),
        pltpu.VMEM((rows, columns), bf16),
        pltpu.VMEM((rows, slots, kv_width), bf16),
        pltpu.VMEM((rows, slots, kv_width), bf16),
        pltpu.VMEM((rows, kv_width), bf16),
        pltpu.VMEM((rows, kv_width), bf16),
        pltpu.VMEM((pages * rank, features), bf16),
        pltpu.VMEM((pages * rank, columns), bf16),
        pltpu.SMEM(cache_len.shape, jnp.int32),
        pltpu.SMEM(active_slots.shape, jnp.int32),
        pltpu.SMEM((batches, each), jnp.int32),
        pltpu.VMEM((rows, features), bf16),
        pltpu.VMEM((batches, tps, sets, each, LANES), f32),
        pltpu.VMEM((batches, reps, rows, columns // 2), bf16),
        pltpu.VMEM((batches, reps, rows, columns // 2), f32),
        pltpu.VMEM((batches, reps, rows, columns // 2), bf16),
        pltpu.VMEM((chunks, rows * HEADS_PER_GROUP, HEAD_SIZE), f32),
        pltpu.VMEM((chunks, rows * HEADS_PER_GROUP, HEAD_SIZE), f32),
        pltpu.VMEM((chunks * each * HEADS_PER_GROUP, HEAD_SIZE), f32),
        pltpu.VMEM((chunks * each * HEADS_PER_GROUP, HEAD_SIZE), f32),
        pltpu.VMEM((rows, columns), f32),
        pltpu.VMEM((rows, columns), bf16),
        dma((11,)),
        dma,
        dma((batches, 2, reps)),
        dma((batches, 2, reps)),
        dma((batches, tps)),
        dma((batches, tps)),
        dma((batches, 2, reps)),
        dma((batches, 2, reps)),
    ]
    anywhere = pl.BlockSpec(memory_space=pl.ANY)
    out = pl.pallas_call(
        functools.partial(kernel, reps, tps, active_slots.shape[1], rank),
        out_shape=jax.ShapeDtypeStruct((rows, columns), bf16),
        in_specs=[anywhere] * 11,
        out_specs=anywhere,
        scratch_shapes=scratch,
        compiler_params=pltpu.CompilerParams(
            collective_id=0, has_side_effects=True, vmem_limit_bytes=60 * 1024 * 1024
        ),
    )(
        row_states.reshape(rows, features),
        q_base.reshape(rows, columns),
        cache_k.reshape(rows, slots, kv_width),
        value_slots.reshape(rows, slots, kv_width),
        current_key.reshape(rows, kv_width),
        current_value.reshape(rows, kv_width),
        cache_len,
        pool_a.reshape(pages * rank, features),
        pool_b.reshape(pages * rank, columns),
        active_slots,
        row_adapter.reshape(batches, each),
    )
    return out.reshape(batches, each, columns)


def solution(mesh):
    placed = (
        P(None, ("groups", "rep"), "tp"),
        P(None, ("groups", "rep"), "tp"),
        P(None, ("groups", "rep"), None, "tp"),
        P(None, ("groups", "rep"), None, "tp"),
        P(None, ("groups", "rep"), "tp"),
        P(None, ("groups", "rep"), "tp"),
        P(None, ("groups", "rep")),
        P("rep", None, "tp"),
        P("rep", None, "tp"),
        P(None, ("groups", "rep")),
        P(None, ("groups", "rep"), None),
    )
    return jax.shard_map(
        functools.partial(body, mesh.shape["rep"], mesh.shape["tp"]),
        mesh=mesh,
        in_specs=placed,
        out_specs=P(None, ("groups", "rep"), "tp"),
        check_vma=False,
    )
```

```python
import functools

import jax
import jax.numpy as jnp
from jax import lax
from jax.experimental import pallas as pl
from jax.experimental.pallas import tpu as pltpu
from jax.sharding import PartitionSpec as P

HEAD_SIZE = 128
HEADS_PER_GROUP = 8
LANES = 128
MESH = pl.DeviceIdType.MESH


def kernel(
    reps,
    tps,
    per_owner,
    rank,
    x_hbm,
    q_hbm,
    k_hbm,
    v_hbm,
    ck_hbm,
    cv_hbm,
    len_hbm,
    a_hbm,
    b_hbm,
    act_hbm,
    ad_hbm,
    out_hbm,
    xbuf,
    qbuf,
    kbuf,
    vbuf,
    ckbuf,
    cvbuf,
    abuf,
    bbuf,
    len_s,
    act_s,
    ad_s,
    xs,
    pbuf,
    dsend,
    down,
    drecv,
    kcb,
    vcb,
    qs,
    os,
    wide_out,
    obuf,
    load_sem,
    out_sem,
    x_send,
    x_recv,
    p_send,
    p_recv,
    d_send,
    d_recv,
):
    rows, features = x_hbm.shape
    half = rows // len_hbm.shape[0]
    slots = k_hbm.shape[1]
    page_lanes = a_hbm.shape[0]
    width = HEADS_PER_GROUP * HEAD_SIZE
    chunks = q_hbm.shape[1] // width
    lane_groups = LANES // rank
    lane_blocks = page_lanes // LANES
    batches = len_hbm.shape[0]
    sets = pbuf.shape[2]
    fold = xbuf.shape[3]
    side_width = chunks * width // 2
    rest = features - fold
    scale = HEAD_SIZE ** (-0.5)
    last = reps - 1
    me = lax.axis_index("rep")
    mt = lax.axis_index("tp")

    def tp_at(step):
        return lax.rem(mt + step, tps)

    barrier = pltpu.get_barrier_semaphore()
    for k in range(1, reps):
        pl.semaphore_signal(
            barrier, inc=1, device_id={"rep": lax.rem(me + k, reps)}, device_id_type=MESH
        )
    for j in range(1, tps):
        pl.semaphore_signal(barrier, inc=1, device_id={"tp": tp_at(j)}, device_id_type=MESH)

    pairs = [
        (ad_hbm, ad_s),
        (x_hbm, xs),
        (act_hbm, act_s),
        (a_hbm, abuf),
        (b_hbm, bbuf),
        (q_hbm, qbuf),
        (ck_hbm, ckbuf),
        (cv_hbm, cvbuf),
        (len_hbm, len_s),
        (k_hbm, kbuf),
        (v_hbm, vbuf),
    ]
    loads = [
        pltpu.make_async_copy(src, dst, load_sem.at[i]) for i, (src, dst) in enumerate(pairs)
    ]
    for load in loads:
        load.start()
    ld_ad, ld_x, ld_act, ld_a, ld_b, ld_q, ld_ck, ld_cv, ld_len, ld_k, ld_v = loads

    row_id = lax.broadcasted_iota(jnp.int32, (rows, LANES), 0)
    lane_group = lax.broadcasted_iota(jnp.int32, (half, LANES), 1) // rank

    ld_ad.wait()
    entry = jnp.zeros((rows, LANES), jnp.int32)
    for n in range(rows):
        entry = jnp.where(row_id == n, ad_s[n // half, n % half], entry)
    entry = entry.astype(jnp.float32)
    ld_x.wait()
    for w in range(batches):
        mine = slice(w * half, (w + 1) * half)
        states = xs[...].astype(jnp.float32)[mine]
        below = [states[:, fold:], entry[mine]]
        if rest + LANES < fold:
            below.append(jnp.zeros((half, fold - rest - LANES), jnp.float32))
        folded = jnp.concatenate([states[:, :fold], jnp.concatenate(below, axis=1)], axis=0)
        xbuf[w, me] = folded.astype(jnp.bfloat16)

    pl.semaphore_wait(barrier, last + tps - 1)

    def reaches(side, step):
        return me + step <= last if side > 0 else me - step >= 0

    def arrives(side, step):
        return me - step >= 0 if side > 0 else me + step <= last

    def row_copy(w, side, step, peer, slot):
        return pltpu.make_async_remote_copy(
            src_ref=xbuf.at[w, slot],
            dst_ref=xbuf.at[w, slot],
            send_sem=x_send.at[w, (side + 1) // 2, step],
            recv_sem=x_recv.at[w, (side + 1) // 2, step],
            device_id={"rep": peer},
            device_id_type=MESH,
        )

    for w in range(batches):
        for step in range(last, 0, -1):
            for side in (1, -1):

                @pl.when(reaches(side, step))
                def _():
                    row_copy(w, side, step, me + side * step, me).start()

    for w in range(batches):
        drecv[w, me] = jnp.zeros((rows, side_width), jnp.bfloat16)

    ld_act.wait()
    ld_a.wait()

    def shrink_dot(block):
        return lax.dot_general(
            block, abuf[...], (((1,), (1,)), ((), ())), preferred_element_type=jnp.float32
        )

    ld_ck.wait()
    ld_cv.wait()
    for c in range(chunks):
        head = slice(c * HEAD_SIZE, (c + 1) * HEAD_SIZE)
        keys = ckbuf[:, head].astype(jnp.float32)
        values = cvbuf[:, head].astype(jnp.float32)
        for n in range(rows):
            place = slice(n * HEADS_PER_GROUP, (n + 1) * HEADS_PER_GROUP)
            shape = (HEADS_PER_GROUP, HEAD_SIZE)
            kcb[c, place, :] = jnp.broadcast_to(keys[n : n + 1, :], shape)
            vcb[c, place, :] = jnp.broadcast_to(values[n : n + 1, :], shape)

    group_f = lane_group.astype(jnp.float32)
    ld_b.wait()

    def shrink_part(w):
        for step in range(1, reps):
            for side in (1, -1):

                @pl.when(arrives(side, step))
                def _():
                    row_copy(w, side, step, me - side * step, me - side * step).wait_recv()

        states, entries = [], []
        for k in range(reps):
            folded = xbuf[w, k].astype(jnp.float32)
            states.append(jnp.concatenate([folded[:half], folded[half:, :rest]], axis=1))
            entries.append(folded[half:, rest : rest + LANES])
        products = shrink_dot(jnp.concatenate(states, axis=0).astype(jnp.bfloat16))
        pages = []
        packed = [jnp.zeros((half, LANES), jnp.float32) for _ in range(sets)]
        for k in range(reps):
            product = products[k * half : (k + 1) * half]
            page = jnp.full((half, LANES), -1.0, jnp.float32)
            for c in range(per_owner):
                mine = (me * per_owner + c).astype(jnp.float32)
                page = jnp.where(entries[k] == mine, act_s[w, c].astype(jnp.float32), page)
            pages.append(page)
            kept = jnp.zeros((half, LANES), jnp.float32)
            for b in range(lane_blocks):
                kept = kept + jnp.where(
                    page == group_f + float(b * lane_groups),
                    product[:, b * LANES : (b + 1) * LANES],
                    0.0,
                )
            turn = LANES // 2
            while turn >= rank:
                kept = kept + pltpu.roll(kept, turn, 1)
                turn //= 2
            s, g = divmod(k, lane_groups)
            packed[s] = jnp.where(lane_group == g, kept, packed[s])
        for s in range(sets):
            pbuf[w, 0, s] = packed[s]
        copies = []
        for j in range(1, tps):
            copy = pltpu.make_async_remote_copy(
                src_ref=pbuf.at[w, 0],
                dst_ref=pbuf.at[w, j],
                send_sem=p_send.at[w, j],
                recv_sem=p_recv.at[w, j],
                device_id={"tp": tp_at(j)},
                device_id_type=MESH,
            )
            copy.start()
            copies.append(copy)
        return pages, copies

    def delta_copy(w, side, step, peer, slot):
        return pltpu.make_async_remote_copy(
            src_ref=dsend.at[w, peer],
            dst_ref=drecv.at[w, slot],
            send_sem=d_send.at[w, (side + 1) // 2, step],
            recv_sem=d_recv.at[w, (side + 1) // 2, step],
            device_id={"rep": peer},
            device_id_type=MESH,
        )

    def expand_part(w, pages, copies):
        for copy in copies:
            copy.wait_recv()
        spread = []
        for k in range(reps):
            s, g = divmod(k, lane_groups)
            if g == 0:
                total = pbuf[w, 0, s]
                for j in range(1, tps):
                    total = total + pbuf[w, j, s]
            shrink = jnp.where(lane_group == g, total, 0.0)
            turn = LANES // 2
            while turn >= rank:
                shrink = shrink + pltpu.roll(shrink, turn, 1)
                turn //= 2
            spread.append(
                jnp.concatenate(
                    [
                        jnp.where(pages[k] == group_f + float(b * lane_groups), shrink, 0.0)
                        for b in range(lane_blocks)
                    ],
                    axis=1,
                )
            )
        spread = jnp.concatenate(spread, axis=0).astype(jnp.bfloat16)
        sides = [
            jnp.dot(
                spread,
                bbuf[:, i * side_width : (i + 1) * side_width],
                preferred_element_type=jnp.float32,
            )
            for i in range(2)
        ]
        for k in range(reps):
            block = jnp.concatenate([side[k * half : (k + 1) * half] for side in sides], axis=0)
            down[w, k] = block
            dsend[w, k] = block.astype(jnp.bfloat16)
        for step in range(last, 0, -1):
            for side in (1, -1):

                @pl.when(reaches(side, step))
                def _():
                    delta_copy(w, side, step, me + side * step, me).start()

    shrunk = [shrink_part(w) for w in range(batches)]
    for w in range(batches):
        expand_part(w, *shrunk[w])

    ld_q.wait()
    ld_len.wait()
    ld_k.wait()
    ld_v.wait()
    slot_id = lax.broadcasted_iota(jnp.int32, (HEADS_PER_GROUP, slots), 1)
    for w in range(batches):
        for step in range(1, reps):
            for side in (1, -1):

                @pl.when(arrives(side, step))
                def _():
                    delta_copy(w, side, step, me - side * step, me - side * step).wait_recv()

        delta = down[w, me]
        for k in range(reps):
            delta = delta + drecv[w, k].astype(jnp.float32)
        delta = jnp.concatenate([delta[:half], delta[half:]], axis=1)
        base = qbuf[...].astype(jnp.float32)[w * half : (w + 1) * half]
        queries = (base + delta).astype(jnp.bfloat16).astype(jnp.float32)
        pairs = [(c, n) for c in range(chunks) for n in range(half)]

        def place(c, n):
            start = (c * half + n) * HEADS_PER_GROUP
            return slice(start, start + HEADS_PER_GROUP)

        def wide(n):
            start = (w * half + n) * HEADS_PER_GROUP
            return slice(start, start + HEADS_PER_GROUP)

        for c in range(chunks):
            for h in range(HEADS_PER_GROUP):
                first = c * width + h * HEAD_SIZE
                qs[pl.ds(c * half * HEADS_PER_GROUP + h, half, stride=HEADS_PER_GROUP), :] = queries[
                    :, first : first + HEAD_SIZE
                ]
        scores, owns = [], []
        for c, n in pairs:
            query = qs[place(c, n), :]
            score = lax.dot_general(
                query.astype(jnp.bfloat16),
                kbuf[w * half + n, :, c * HEAD_SIZE : (c + 1) * HEAD_SIZE],
                (((1,), (1,)), ((), ())),
                preferred_element_type=jnp.float32,
            )
            owns.append(jnp.sum(query * kcb[c, wide(n), :], axis=1, keepdims=True) * scale)
            scores.append(jnp.where(slot_id < len_s[w, n], score * scale, -jnp.inf))
        weights, own_weights, denominators = [], [], []
        for score, own in zip(scores, owns):
            highest = jnp.maximum(jnp.max(score, axis=1, keepdims=True), own)
            weight = jnp.exp(score - highest)
            own_weight = jnp.exp(own - highest)
            denominators.append(jnp.sum(weight, axis=1, keepdims=True) + own_weight)
            weights.append(weight)
            own_weights.append(own_weight.astype(jnp.bfloat16).astype(jnp.float32))
        joint = [
            jnp.dot(
                jnp.concatenate([weights[c * half + n] for c in range(chunks)], axis=0).astype(
                    jnp.bfloat16
                ),
                vbuf[w * half + n],
                preferred_element_type=jnp.float32,
            )
            for n in range(half)
        ]
        for i, (c, n) in enumerate(pairs):
            mixed = joint[n][
                c * HEADS_PER_GROUP : (c + 1) * HEADS_PER_GROUP, c * HEAD_SIZE : (c + 1) * HEAD_SIZE
            ]
            mixed = mixed + own_weights[i] * vcb[c, wide(n), :]
            os[place(c, n), :] = mixed / denominators[i]
        for c in range(chunks):
            for h in range(HEADS_PER_GROUP):
                first = c * width + h * HEAD_SIZE
                wide_out[w * half : (w + 1) * half, first : first + HEAD_SIZE] = os[
                    pl.ds(c * half * HEADS_PER_GROUP + h, half, stride=HEADS_PER_GROUP), :
                ]
    obuf[...] = wide_out[...].astype(jnp.bfloat16)
    out_copy = pltpu.make_async_copy(obuf, out_hbm, out_sem)
    out_copy.start()

    for _, copies in shrunk:
        for copy in copies:
            copy.wait_send()
    for step in range(1, reps):
        for side in (1, -1):

            @pl.when(reaches(side, step))
            def _():
                for w in range(batches):
                    row_copy(w, side, step, me + side * step, me).wait_send()
                    delta_copy(w, side, step, me + side * step, me).wait_send()

    out_copy.wait()


def body(
    reps,
    tps,
    row_states,
    q_base,
    cache_k,
    value_slots,
    current_key,
    current_value,
    cache_len,
    pool_a,
    pool_b,
    active_slots,
    row_adapter,
):
    batches, each, features = row_states.shape
    rows = batches * each
    columns = q_base.shape[2]
    slots, kv_width = cache_k.shape[2:]
    pages, rank = pool_a.shape[:2]
    width = HEADS_PER_GROUP * HEAD_SIZE
    chunks = columns // width
    sets = -(-reps * rank // LANES)
    fold = (features + 2 * LANES) // (2 * LANES) * LANES
    bf16, f32 = jnp.bfloat16, jnp.float32
    dma = pltpu.SemaphoreType.DMA
    scratch = [
        pltpu.VMEM((batches, reps, rows, fold), bf16),
        pltpu.VMEM((rows, columns), bf16),
        pltpu.VMEM((rows, slots, kv_width), bf16),
        pltpu.VMEM((rows, slots, kv_width), bf16),
        pltpu.VMEM((rows, kv_width), bf16),
        pltpu.VMEM((rows, kv_width), bf16),
        pltpu.VMEM((pages * rank, features), bf16),
        pltpu.VMEM((pages * rank, columns), bf16),
        pltpu.SMEM(cache_len.shape, jnp.int32),
        pltpu.SMEM(active_slots.shape, jnp.int32),
        pltpu.SMEM((batches, each), jnp.int32),
        pltpu.VMEM((rows, features), bf16),
        pltpu.VMEM((batches, tps, sets, each, LANES), f32),
        pltpu.VMEM((batches, reps, rows, columns // 2), bf16),
        pltpu.VMEM((batches, reps, rows, columns // 2), f32),
        pltpu.VMEM((batches, reps, rows, columns // 2), bf16),
        pltpu.VMEM((chunks, rows * HEADS_PER_GROUP, HEAD_SIZE), f32),
        pltpu.VMEM((chunks, rows * HEADS_PER_GROUP, HEAD_SIZE), f32),
        pltpu.VMEM((chunks * each * HEADS_PER_GROUP, HEAD_SIZE), f32),
        pltpu.VMEM((chunks * each * HEADS_PER_GROUP, HEAD_SIZE), f32),
        pltpu.VMEM((rows, columns), f32),
        pltpu.VMEM((rows, columns), bf16),
        dma((11,)),
        dma,
        dma((batches, 2, reps)),
        dma((batches, 2, reps)),
        dma((batches, tps)),
        dma((batches, tps)),
        dma((batches, 2, reps)),
        dma((batches, 2, reps)),
    ]
    anywhere = pl.BlockSpec(memory_space=pl.ANY)
    out = pl.pallas_call(
        functools.partial(kernel, reps, tps, active_slots.shape[1], rank),
        out_shape=jax.ShapeDtypeStruct((rows, columns), bf16),
        in_specs=[anywhere] * 11,
        out_specs=anywhere,
        scratch_shapes=scratch,
        compiler_params=pltpu.CompilerParams(
            collective_id=0, has_side_effects=True, vmem_limit_bytes=60 * 1024 * 1024
        ),
    )(
        row_states.reshape(rows, features),
        q_base.reshape(rows, columns),
        cache_k.reshape(rows, slots, kv_width),
        value_slots.reshape(rows, slots, kv_width),
        current_key.reshape(rows, kv_width),
        current_value.reshape(rows, kv_width),
        cache_len,
        pool_a.reshape(pages * rank, features),
        pool_b.reshape(pages * rank, columns),
        active_slots,
        row_adapter.reshape(batches, each),
    )
    return out.reshape(batches, each, columns)


def solution(mesh):
    placed = (
        P(None, ("groups", "rep"), "tp"),
        P(None, ("groups", "rep"), "tp"),
        P(None, ("groups", "rep"), None, "tp"),
        P(None, ("groups", "rep"), None, "tp"),
        P(None, ("groups", "rep"), "tp"),
        P(None, ("groups", "rep"), "tp"),
        P(None, ("groups", "rep")),
        P("rep", None, "tp"),
        P("rep", None, "tp"),
        P(None, ("groups", "rep")),
        P(None, ("groups", "rep"), None),
    )
    return jax.shard_map(
        functools.partial(body, mesh.shape["rep"], mesh.shape["tp"]),
        mesh=mesh,
        in_specs=placed,
        out_specs=P(None, ("groups", "rep"), "tp"),
        check_vma=False,
    )
```
